256 devices in a mesh: blk: 64 (over z, x, core), grp: 4 (over y).
Axes of the slice: x: 4, y: 4, z: 8, core: 2. Of those that a mesh axis runs over, the one named last changes fastest.
Arguments:
- embeddings: bfloat16 [131072, 4096], P(('blk', 'grp')), may hold values from -40 to 40, as said below
- cluster_sizes: int32 [128], replicated, may hold values from 1 to 4096, 131072 in all
- sign_bits: int32 [4096], replicated, may hold values from 0 to 1
- sample_cols: int32 [1024], replicated, may hold values from 0 to 4095
Outputs:
- nearest: float32 [131072], P(('blk', 'grp'))
The draws below stay inside these ranges and needn't reach their ends.
Inputs may be any that keep to these rules, and one draw needn't show every extreme that they name: embeddings: rows mix independent vectors with earlier rows at random weights. `cluster_sizes`: rows of each cluster in order; they sum to 131072, the largest is exactly 4096.
All inputs are finite; a program needn't handle non-finite values.
Results may differ from the reference program's by a relative error of at most 0.00043.
Values may be sent and summed in bfloat16 or wider, within the bound.
A program may use at most 64 MiB of HBM per device.

```python
import math
import jax
import jax.numpy as jnp
import numpy as np
from jax import lax

D = 4096
K = 1024
HB = 256
BLOCK = 512
ROWS = 131072
CLUSTERS = 128
MOST_ROWS = 4096


def draw_embeddings(key, part):
    basic_key, offset_key, weight_key = jax.random.split(jax.random.fold_in(key, 11), 3)
    basic_rows = jax.random.normal(basic_key, (ROWS, D), jnp.float32)
    offsets = jax.random.randint(offset_key, (ROWS,), 1, MOST_ROWS)
    partner = jnp.maximum(jnp.arange(ROWS, dtype=jnp.int32) - offsets, 0)
    weights = jax.random.uniform(weight_key, (ROWS, 1), jnp.float32, 0.0, 0.95)
    mixed = weights * basic_rows[partner] + jnp.sqrt(1.0 - weights * weights) * basic_rows
    return jnp.clip(mixed, -40.0, 40.0).astype(jnp.bfloat16)


def place_ends(values, stream_key, least, high):
    spot = [jax.random.randint(jax.random.fold_in(stream_key, axis), (), 0, length) for axis, length in enumerate(values.shape)]
    main_axis = values.shape.index(max(values.shape))
    neighbour = spot[:main_axis] + [(spot[main_axis] + 1) % values.shape[main_axis]] + spot[main_axis + 1:]
    return values.at[tuple(spot)].set(least).at[tuple(neighbour)].set(high)


def length_profile(number_of, total, limit, skew):
    portions = [(1 << 20) // math.isqrt(standing ** skew) + 1 for standing in range(2, number_of + 1)]
    rest, holding = total - limit - (number_of - 1), [1] * (number_of - 1)
    while rest > 0:
        free = [i for i in range(number_of - 1) if holding[i] < limit]
        mass, remaining = sum([portions[i] for i in free]), rest
        for i in free:
            extra = min(limit - holding[i], max(1, remaining * portions[i] // mass), rest)
            holding[i] = holding[i] + extra
            rest = rest - extra
    return np.array([limit] + holding)


def ragged_sizes(own_key, number_of, total, bound, slope):
    if number_of == 2:
        one = jax.random.randint(own_key, (), max(1, total - bound), min(bound, total - 1) + 1)
        return jnp.stack([one, total - one])
    tallies = jnp.asarray(length_profile(number_of, total, bound, slope), jnp.int32)
    pairs = (number_of - 1) // 2
    giver, sink = tallies[1:1 + 2 * pairs:2], tallies[2:2 + 2 * pairs:2]
    slack = jnp.minimum(giver - 1, bound - sink)
    passed = jax.random.randint(jax.random.fold_in(own_key, 1), (pairs,), 0, 1 << 20) % (slack + 1)
    tallies = tallies.at[1:1 + 2 * pairs:2].set(giver - passed).at[2:2 + 2 * pairs:2].set(sink + passed)
    return tallies[jax.random.permutation(jax.random.fold_in(own_key, 2), number_of)]


def setup_inputs(seed: int = 0) -> dict:
    arg_keys = jax.random.split(jax.random.key(seed), 5)
    embeddings = draw_embeddings(jax.random.fold_in(arg_keys[4], 71), 0)
    cluster_sizes = ragged_sizes(arg_keys[1], CLUSTERS, ROWS, MOST_ROWS, 2).astype(jnp.int32)
    sign_bits = place_ends(jax.random.randint(arg_keys[2], (D,), 0, 2), jax.random.fold_in(arg_keys[2], 1), 0, 1).astype(jnp.int32)
    sample_cols = place_ends(jax.random.randint(arg_keys[3], (K,), 0, D), jax.random.fold_in(arg_keys[3], 1), 0, D - 1).astype(jnp.int32)
    return {"embeddings": embeddings, "cluster_sizes": cluster_sizes, "sign_bits": sign_bits, "sample_cols": sample_cols}


def hadamard(order):
    indices = jnp.arange(order, dtype=jnp.int32)
    parity = jnp.zeros((order, order), jnp.int32)
    for place in range(order.bit_length() - 1):
        parity = parity + (indices[:, None] >> place & 1) * (indices[None, :] >> place & 1)
    return jnp.where(parity % 2 == 0, 1.0, -1.0).astype(jnp.bfloat16)

def sketch_rows(rows_emb, sign_bits, sample_cols):
    count = rows_emb.shape[0]
    flips = (2 * sign_bits - 1).astype(jnp.bfloat16)
    flipped = rows_emb * flips[None, :]
    table = hadamard(HB).astype(jnp.float32)
    mixed = jnp.einsum('rbi,ij->rbj', flipped.astype(jnp.float32).reshape(count, D // HB, HB), table).reshape(count, D)
    picked = jnp.take(mixed, sample_cols, axis=1)
    scale = lax.rsqrt(lax.optimization_barrier(jnp.sum(picked * picked, axis=1, keepdims=True)) + 1e-06)
    return (picked * scale).astype(jnp.bfloat16)

def cluster_of(first_row, count, ends):
    rows = first_row + jnp.arange(count, dtype=jnp.int32)
    return lax.optimization_barrier(jnp.sum((ends[None, :] <= rows[:, None]).astype(jnp.int32), axis=1))

def cosines(left, right):
    return lax.dot_general(left, right, (((1,), (1,)), ((), ())), preferred_element_type=jnp.float32)

def reference(embeddings, cluster_sizes, sign_bits, sample_cols):
    count_blocks = ROWS // BLOCK
    stacked = embeddings.reshape(count_blocks, BLOCK, D)
    sketches = lax.map(lambda rows_emb: sketch_rows(rows_emb, sign_bits, sample_cols), stacked)
    ends = jnp.cumsum(cluster_sizes).astype(jnp.int32)
    all_ids = cluster_of(jnp.int32(0), ROWS, ends).reshape(count_blocks, BLOCK)
    first_ids = all_ids[:, 0]
    last_ids = all_ids[:, BLOCK - 1]
    reach_blocks = (MOST_ROWS - 2) // BLOCK + 1
    positions = jnp.arange(BLOCK, dtype=jnp.int32)
    nearest = jnp.full((count_blocks, BLOCK), -1.0, jnp.float32)

    def visit(index, nearest):
        own = sketches[index]
        own_ids = all_ids[index]
        scores = cosines(own, own)
        paired = (own_ids[:, None] == own_ids[None, :]) & (positions[:, None] != positions[None, :])
        masked = jnp.where(paired, scores, -1.0)
        nearest = nearest.at[index].set(jnp.maximum(nearest[index], lax.optimization_barrier(jnp.max(masked, axis=1))))
        for offset in range(1, reach_blocks + 1):
            other = jnp.maximum(index - offset, 0).astype(jnp.int32)
            needed = jnp.logical_and(index - offset >= 0, last_ids[other] == first_ids[index])

            def compute(current):
                other_scores = cosines(own, sketches[other])
                other_pair = own_ids[:, None] == all_ids[other][None, :]
                other_mask = jnp.where(other_pair, other_scores, -1.0)
                current = current.at[index].set(jnp.maximum(current[index], lax.optimization_barrier(jnp.max(other_mask, axis=1))))
                return current.at[other].set(jnp.maximum(current[other], lax.optimization_barrier(jnp.max(other_mask, axis=0))))
            nearest = lax.cond(needed, compute, lambda current: current, nearest)
        return nearest
    nearest = lax.fori_loop(0, count_blocks, visit, nearest)
    return nearest.reshape(ROWS)
```

```python
import functools

import jax
import jax.numpy as jnp
from jax import lax
from jax.experimental import pallas as pl
from jax.experimental.pallas import tpu as pltpu
from jax.sharding import PartitionSpec as P

HB = 256
MESH = pl.DeviceIdType.MESH
F32 = jnp.float32
BF16 = jnp.bfloat16

A0, A1, A2, X0, B0, Y0, Z, W = range(8)
KINDS = 8


def parity_sign(bits):
    bits = bits ^ (bits >> 2)
    bits = bits ^ (bits >> 1)
    return (1 - 2 * (bits & 1)).astype(F32)


def kernel(blocks, groups, chunks, emb_ref, sizes_ref, sign_ref, cols_ref, out_ref, held, x_in, table, picked, row_best,
           lane_best, row_id, lane_id, landed, load_sem, send_sem, recv_sem, back_send, back_recv):
    rows, width = x_in.shape
    kept = table.shape[1]
    part = rows // chunks
    columns = blocks // 2
    blk = lax.axis_index("blk")
    y = lax.axis_index("grp")
    core = lax.rem(blk, 2)
    t = blk // 2
    step = 2 * core - 1

    def wrap(v, n):
        return lax.rem(v + 2 * n, n)

    y_on, y_back, y_two = wrap(y + step, groups), wrap(y - step, groups), wrap(y + 2, groups)
    t_on, t_back = wrap(t + step, columns), wrap(t - step, columns)
    own_on, own_back = 2 * t_on + core, 2 * t_back + core
    other, other_on = 2 * t + 1 - core, 2 * t_on + 1 - core
    z_to = 2 * wrap(t + core, columns) + 1 - core
    z_from = 2 * wrap(t - 1 + core, columns) + 1 - core

    partners = [
        (blk, y_on), (blk, y_back), (blk, y_two), (own_on, y), (own_back, y), (other, y), (other_on, y),
        (z_to, y_on), (z_from, y_back),
    ]
    barrier = pltpu.get_barrier_semaphore()
    for device in partners:
        pl.semaphore_signal(barrier, inc=1, device_id=device, device_id_type=MESH)

    loads = [
        pltpu.make_async_copy(emb_ref.at[pl.ds(c * part, part)], x_in.at[pl.ds(c * part, part)], load_sem.at[c])
        for c in range(chunks)
    ]
    for load in loads:
        load.start()

    cols = cols_ref[...]
    nibble = lax.broadcasted_iota(jnp.int32, (16, kept), 0)
    low = parity_sign(nibble & (cols & 15)).astype(F32)
    high = parity_sign(nibble & ((cols >> 4) & 15)).astype(F32)
    for u in range(16):
        picked[pl.ds(u * 16, 16), :] = low * high[u:u + 1, :]

    def fill(run, carry):
        chosen = jnp.where((cols >> 8) == run, 1.0, 0.0)
        table[pl.ds(pl.multiple_of(run * HB, HB), HB), :] = (picked[pl.ds(0, HB), :] * chosen).astype(BF16)
        return carry

    lax.fori_loop(0, width // HB, fill, 0)

    n_clusters = sizes_ref.shape[1]
    at = lax.broadcasted_iota(jnp.int32, (n_clusters, n_clusters), 0)
    upto = lax.broadcasted_iota(jnp.int32, (n_clusters, n_clusters), 1)
    ends = jnp.sum(jnp.where(upto <= at, sizes_ref[...], 0), axis=1, keepdims=True)

    def number(column, of_core, place):
        return (2 * column + of_core) * groups + place

    numbers = [
        number(t, core, y), number(t, core, y_back), number(t, core, y_two), number(t_back, core, y),
        number(t, 1 - core, y), number(t_on, 1 - core, y), number(wrap(t + core, columns), 1 - core, y_on),
        number(wrap(t - 1, columns), 1, groups - 1),
    ]
    for slot, block in enumerate(numbers):
        which = block * rows + lax.broadcasted_iota(jnp.int32, (n_clusters, rows), 1)
        ids = jnp.sum(jnp.where(ends <= which, 1.0, 0.0), axis=0, keepdims=True)
        lane_id[pl.ds(slot * 8, 8), :] = jnp.broadcast_to(ids, (8, rows))
        if slot in (A0, A1, A2, B0):
            row_id[pl.ds(slot * rows, rows), :] = jnp.broadcast_to(ids, (128, rows)).T
    row_best[...] = jnp.full_like(row_best, -1.0)
    lane_best[...] = jnp.full_like(lane_best, -1.0)

    def copy(source, target, c, device):
        return pltpu.make_async_remote_copy(
            src_ref=held.at[pl.ds(source * rows + c * part, part)],
            dst_ref=held.at[pl.ds(target * rows + c * part, part)],
            send_sem=send_sem.at[target, c],
            recv_sem=recv_sem.at[target, c],
            device_id=device,
            device_id_type=MESH,
        )

    def tile(left, left_at, count, right, right_at, lanes, own):
        rows_at = left * rows + left_at
        if not isinstance(rows_at, int):
            rows_at = pl.multiple_of(rows_at, 128)
        other_at = right * rows + right_at
        if not isinstance(other_at, int):
            other_at = pl.multiple_of(other_at, 128)
        scores = lax.dot_general(
            held[pl.ds(rows_at, count), :], held[pl.ds(other_at, lanes), :], (((1,), (1,)), ((), ())),
            preferred_element_type=F32,
        )
        left_ids = row_id[pl.ds(rows_at, count), :]
        best = row_best[pl.ds(rows_at, count), :]
        lane_row = right * 8 if isinstance(right, int) else pl.multiple_of(right * 8, 8)
        for j in range(lanes // 128):
            span = pl.ds(right_at + j * 128, 128)
            paired = left_ids == lane_id[pl.ds(lane_row, 8), span][0:1, :]
            if own:
                mine = left_at + lax.broadcasted_iota(jnp.int32, (count, 128), 0)
                theirs = right_at + j * 128 + lax.broadcasted_iota(jnp.int32, (count, 128), 1)
                paired = paired & (mine != theirs)
            masked = jnp.where(paired, scores[:, j * 128:(j + 1) * 128], -1.0)
            best = jnp.maximum(best, masked)
            if not own:
                lane_best[pl.ds(lane_row, 8), span] = jnp.maximum(
                    lane_best[pl.ds(lane_row, 8), span], jnp.max(masked.reshape(count // 8, 8, 128), axis=0)
                )
        row_best[pl.ds(rows_at, count), :] = best

    def tiles(left, right, left_part=None, right_part=None, own=False):
        for lc in range(chunks) if left_part is None else (left_part,):
            for rc in range(chunks) if right_part is None else (right_part,):
                tile(left, lc * part, part, right, rc * part, part, own)

    def close(slot):
        turned = row_best[pl.ds(slot * rows, rows), :].T
        lane_best[pl.ds(slot * 8, 8), :] = jnp.maximum(
            lane_best[pl.ds(slot * 8, 8), :], jnp.max(turned.reshape(16, 8, rows), axis=0)
        )

    signs = (2 * sign_ref[...] - 1).astype(F32).astype(BF16)
    sent = []
    for c in range(chunks):
        loads[c].wait()
        here = pl.ds(c * part, part)
        x_in[here, :] = x_in[here, :] * signs

        def project(n, total):
            span = pl.ds(pl.multiple_of(n * 256, 256), 256)
            some = jnp.dot(x_in[here, :], table[:, span], preferred_element_type=F32)
            picked[:, span] = some
            return total + some[:, :128] * some[:, :128] + some[:, 128:] * some[:, 128:]

        total = lax.fori_loop(0, kept // 256, project, jnp.zeros((part, 128), F32))
        scale = lax.rsqrt(jnp.sum(total, axis=1, keepdims=True) + 1e-6)
        held[here, :] = (picked[...] * scale).astype(BF16)
        if c == 0:
            pl.semaphore_wait(barrier, len(partners))
        for target, device in ((A1, (blk, y_on)), (X0, (own_on, y)), (B0, (other, y))):
            out = copy(A0, target, c, device)
            out.start()
            sent.append(out)

    tiles(A0, A0, own=True)
    for c in range(chunks):
        copy(A0, B0, c, (other, y)).wait_recv()

    @pl.when(core == 1)
    def _():
        tiles(A0, B0)

    z_core0 = [copy(A1, Z, c, (other_on, y)) for c in range(chunks)]
    z_core1 = [copy(A1, Z, c, (other, y)) for c in range(chunks)]
    w_out = [copy(A1, W, c, (other_on, y)) for c in range(chunks)]
    for c in range(chunks):
        copy(A0, A1, c, (blk, y_on)).wait_recv()
        out = copy(A1, A2, c, (blk, y_on))
        out.start()
        sent.append(out)

        @pl.when(core == 0)
        def _():
            z_core0[c].start()

        @pl.when(core == 1)
        def _():
            z_core1[c].start()

        @pl.when(jnp.logical_and(core == 1, y == 0))
        def _():
            w_out[c].start()

        copy(A0, X0, c, (own_on, y)).wait_recv()
        out = copy(X0, Y0, c, (other, y))
        out.start()
        sent.append(out)
        tiles(A1, A0, left_part=c)
        tiles(A0, X0, right_part=c)
    tiles(A1, X0)
    for c in range(chunks):
        copy(X0, Y0, c, (other, y)).wait_recv()

    @pl.when(core == 0)
    def _():
        tiles(A1, B0)
        tiles(A0, Y0)

    @pl.when(core == 1)
    def _():
        tiles(A1, Y0)

    for c in range(chunks):
        copy(A1, A2, c, (blk, y_on)).wait_recv()
        tiles(A2, A0, left_part=c)
        tiles(A2, X0, left_part=c)

        @pl.when(core == 0)
        def _():
            tiles(A2, Y0, left_part=c)

        @pl.when(core == 1)
        def _():
            tiles(A2, B0, left_part=c)

        copy(A1, Z, c, (other, y)).wait_recv()
        tiles(A2, Z, left_part=c, right_part=c)
        for before in range(c):
            tiles(A2, Z, left_part=c, right_part=before)
            tiles(A2, Z, left_part=before, right_part=c)

    @pl.when(jnp.logical_and(core == 1, y == groups - 1))
    def _():
        tiles(B0, Z)
        close(B0)

    @pl.when(jnp.logical_and(core == 0, y == 0))
    def _():
        for c in range(chunks):
            copy(A1, W, c, (other, y)).wait_recv()
        tiles(B0, W)
        close(B0)

    for slot in (A0, A1, A2):
        close(slot)

    def give(slot, device):
        return pltpu.make_async_remote_copy(
            src_ref=lane_best.at[pl.ds(slot * 8, 8)],
            dst_ref=landed.at[pl.ds(slot * 8, 8)],
            send_sem=back_send.at[slot],
            recv_sem=back_recv.at[slot],
            device_id=device,
            device_id_type=MESH,
        )

    back = [
        give(A1, (blk, y_back)), give(A2, (blk, y_two)), give(X0, (own_back, y)), give(B0, (other, y)),
        give(Y0, (other_on, y)), give(Z, (z_to, y_on)),
    ]
    w_back = give(W, (2 * wrap(t - 1, columns) + 1, groups - 1))
    for out in back:
        out.start()

    @pl.when(jnp.logical_and(core == 0, y == 0))
    def _():
        w_back.start()

    best = lane_best[pl.ds(A0 * 8, 8), :]
    for out, slot in zip(back, (A1, A2, X0, B0, Y0, Z), strict=True):
        out.wait_recv()
        best = jnp.maximum(best, landed[pl.ds(slot * 8, 8), :])
    out_ref[...] = jnp.max(best, axis=0, keepdims=True)

    @pl.when(jnp.logical_and(core == 1, y == groups - 1))
    def _():
        w_back.wait_recv()
        out_ref[...] = jnp.maximum(out_ref[...], jnp.max(landed[pl.ds(W * 8, 8), :], axis=0, keepdims=True))

    for out in (*sent, *back):
        out.wait_send()
    for c in range(chunks):
        z_core0[c].wait_send()

        @pl.when(jnp.logical_and(core == 1, y == 0))
        def _():
            w_out[c].wait_send()

    @pl.when(jnp.logical_and(core == 0, y == 0))
    def _():
        w_back.wait_send()


def solution(mesh):
    blocks, groups = mesh.shape["blk"], mesh.shape["grp"]
    chunks = 2

    def local(embeddings, cluster_sizes, sign_bits, sample_cols):
        rows, width = embeddings.shape
        kept = sample_cols.shape[0]
        vmem = pl.BlockSpec(memory_space=pltpu.VMEM)
        best = pl.pallas_call(
            functools.partial(kernel, blocks, groups, chunks),
            out_shape=jax.ShapeDtypeStruct((1, rows), F32),
            in_specs=[pl.BlockSpec(memory_space=pl.ANY), vmem, vmem, vmem],
            out_specs=vmem,
            scratch_shapes=[
                pltpu.VMEM((8 * rows, kept), BF16),
                pltpu.VMEM((rows, width), BF16),
                pltpu.VMEM((width, kept), BF16),
                pltpu.VMEM((rows // chunks, kept), F32),
                pltpu.VMEM((5 * rows, 128), F32),
                pltpu.VMEM((64, rows), F32),
                pltpu.VMEM((5 * rows, 128), F32),
                pltpu.VMEM((64, rows), F32),
                pltpu.VMEM((64, rows), F32),
                pltpu.SemaphoreType.DMA((chunks,)),
                pltpu.SemaphoreType.DMA((KINDS, chunks)),
                pltpu.SemaphoreType.DMA((KINDS, chunks)),
                pltpu.SemaphoreType.DMA((KINDS,)),
                pltpu.SemaphoreType.DMA((KINDS,)),
            ],
            compiler_params=pltpu.CompilerParams(
                collective_id=0, has_side_effects=True, vmem_limit_bytes=48 * 1024 * 1024
            ),
        )(embeddings, cluster_sizes.reshape(1, -1), sign_bits.reshape(1, -1), sample_cols.reshape(1, -1))
        return best.reshape(rows)

    placed = (P(("blk", "grp"), None), P(), P(), P())
    return jax.shard_map(local, mesh=mesh, in_specs=placed, out_specs=P(("blk", "grp")), check_vma=False)
```

```python
import functools

import jax
import jax.numpy as jnp
from jax import lax
from jax.experimental import pallas as pl
from jax.experimental.pallas import tpu as pltpu
from jax.sharding import PartitionSpec as P

HB = 256
MESH = pl.DeviceIdType.MESH
F32 = jnp.float32
BF16 = jnp.bfloat16

A0, A1, A2, X0, B0, Y0, Z, W = range(8)
KINDS = 8


def parity_sign(bits):
    bits = bits ^ (bits >> 2)
    bits = bits ^ (bits >> 1)
    return (1 - 2 * (bits & 1)).astype(F32)


def kernel(blocks, groups, chunks, emb_ref, sizes_in, sign_in, cols_in, out_ref, sizes_ref, sign_ref, cols_ref, held, x_in,
           table, picked, row_best, lane_best, row_id, lane_id, landed, load_sem, small_sem, send_sem, recv_sem, back_send,
           back_recv):
    rows, width = x_in.shape
    kept = table.shape[1]
    part = rows // chunks
    columns = blocks // 2
    blk = lax.axis_index("blk")
    y = lax.axis_index("grp")
    core = lax.rem(blk, 2)
    t = blk // 2
    step = 2 * core - 1

    def wrap(v, n):
        return lax.rem(v + 2 * n, n)

    y_on, y_back, y_two = wrap(y + step, groups), wrap(y - step, groups), wrap(y + 2, groups)
    t_on, t_back = wrap(t + step, columns), wrap(t - step, columns)
    own_on, own_back = 2 * t_on + core, 2 * t_back + core
    other, other_on = 2 * t + 1 - core, 2 * t_on + 1 - core
    z_to = 2 * wrap(t + core, columns) + 1 - core

    has_on = jnp.logical_and(t + step >= 0, t + step < columns)
    has_back = jnp.logical_and(t - step >= 0, t - step < columns)
    has_z = jnp.logical_or(core == 0, t < columns - 1)

    barrier = pltpu.get_barrier_semaphore()

    def greet(*devices):
        for device in devices:
            pl.semaphore_signal(barrier, inc=1, device_id=device, device_id_type=MESH)

    small = [
        pltpu.make_async_copy(source, target, small_sem.at[i])
        for i, (source, target) in enumerate(((cols_in, cols_ref), (sizes_in, sizes_ref), (sign_in, sign_ref)))
    ]
    for load in small:
        load.start()

    greet((blk, y_on), (blk, y_back), (blk, y_two), (other, y))

    @pl.when(core == 0)
    def _():
        greet((other, y_on))

    @pl.when(core == 1)
    def _():
        greet((other, y_back))

    @pl.when(has_on)
    def _():
        greet((own_on, y), (other_on, y))

    @pl.when(jnp.logical_and(has_on, core == 0))
    def _():
        greet((other_on, y_back))

    @pl.when(jnp.logical_and(has_on, core == 1))
    def _():
        greet((other_on, y_on))

    @pl.when(has_back)
    def _():
        greet((own_back, y))

    loads = [
        pltpu.make_async_copy(emb_ref.at[pl.ds(c * part, part)], x_in.at[pl.ds(c * part, part)], load_sem.at[c])
        for c in range(chunks)
    ]
    for load in loads:
        load.start()

    small[0].wait()
    cols = cols_ref[...]
    nibble = lax.broadcasted_iota(jnp.int32, (16, kept), 0)
    low = parity_sign(nibble & (cols & 15)).astype(F32)
    high = parity_sign(nibble & ((cols >> 4) & 15)).astype(F32)
    for u in range(16):
        picked[pl.ds(u * 16, 16), :] = low * high[u:u + 1, :]

    def fill(run, carry):
        chosen = jnp.where((cols >> 8) == run, 1.0, 0.0)
        table[pl.ds(pl.multiple_of(run * HB, HB), HB), :] = (picked[pl.ds(0, HB), :] * chosen).astype(BF16)
        return carry

    lax.fori_loop(0, width // HB, fill, 0)

    small[1].wait()
    n_clusters = sizes_ref.shape[1]
    at = lax.broadcasted_iota(jnp.int32, (n_clusters, n_clusters), 0)
    upto = lax.broadcasted_iota(jnp.int32, (n_clusters, n_clusters), 1)
    ends = jnp.sum(jnp.where(upto <= at, sizes_ref[...], 0), axis=1, keepdims=True)

    def number(column, of_core, place):
        return (2 * column + of_core) * groups + place

    numbers = [
        number(t, core, y), number(t, core, y_back), number(t, core, y_two), number(t_back, core, y),
        number(t, 1 - core, y), number(t_on, 1 - core, y), number(wrap(t + core, columns), 1 - core, y_on),
        number(wrap(t - 1, columns), 1, groups - 1),
    ]
    for slot, block in enumerate(numbers):
        which = block * rows + lax.broadcasted_iota(jnp.int32, (n_clusters, rows), 1)
        ids = jnp.sum(jnp.where(ends <= which, 1.0, 0.0), axis=0, keepdims=True)
        lane_id[pl.ds(slot * 8, 8), :] = jnp.broadcast_to(ids, (8, rows))
        if slot in (A0, A1, A2, B0):
            row_id[pl.ds(slot * rows, rows), :] = jnp.broadcast_to(ids, (128, rows)).T
    row_best[...] = jnp.full_like(row_best, -1.0)
    lane_best[...] = jnp.full_like(lane_best, -1.0)

    def copy(source, target, c, device):
        return pltpu.make_async_remote_copy(
            src_ref=held.at[pl.ds(source * rows + c * part, part)],
            dst_ref=held.at[pl.ds(target * rows + c * part, part)],
            send_sem=send_sem.at[target, c],
            recv_sem=recv_sem.at[target, c],
            device_id=device,
            device_id_type=MESH,
        )

    def tile(left, left_at, count, right, right_at, lanes, own):
        rows_at = left * rows + left_at
        if not isinstance(rows_at, int):
            rows_at = pl.multiple_of(rows_at, 128)
        other_at = right * rows + right_at
        if not isinstance(other_at, int):
            other_at = pl.multiple_of(other_at, 128)
        scores = lax.dot_general(
            held[pl.ds(rows_at, count), :], held[pl.ds(other_at, lanes), :], (((1,), (1,)), ((), ())),
            preferred_element_type=F32,
        )
        left_ids = row_id[pl.ds(rows_at, count), :]
        best = row_best[pl.ds(rows_at, count), :]
        lane_row = right * 8 if isinstance(right, int) else pl.multiple_of(right * 8, 8)
        for j in range(lanes // 128):
            span = pl.ds(right_at + j * 128, 128)
            paired = left_ids == lane_id[pl.ds(lane_row, 8), span][0:1, :]
            if own:
                mine = left_at + lax.broadcasted_iota(jnp.int32, (count, 128), 0)
                theirs = right_at + j * 128 + lax.broadcasted_iota(jnp.int32, (count, 128), 1)
                paired = paired & (mine != theirs)
            masked = jnp.where(paired, scores[:, j * 128:(j + 1) * 128], -1.0)
            best = jnp.maximum(best, masked)
            if not own:
                lane_best[pl.ds(lane_row, 8), span] = jnp.maximum(
                    lane_best[pl.ds(lane_row, 8), span], jnp.max(masked.reshape(count // 8, 8, 128), axis=0)
                )
        row_best[pl.ds(rows_at, count), :] = best

    def tiles(left, right, left_part=None, right_part=None, own=False):
        for lc in range(chunks) if left_part is None else (left_part,):
            for rc in range(chunks) if right_part is None else (right_part,):
                tile(left, lc * part, part, right, rc * part, part, own)

    def close(slot):
        turned = row_best[pl.ds(slot * rows, rows), :].T
        lane_best[pl.ds(slot * 8, 8), :] = jnp.maximum(
            lane_best[pl.ds(slot * 8, 8), :], jnp.max(turned.reshape(16, 8, rows), axis=0)
        )

    def give(slot, device):
        return pltpu.make_async_remote_copy(
            src_ref=lane_best.at[pl.ds(slot * 8, 8)],
            dst_ref=landed.at[pl.ds(slot * 8, 8)],
            send_sem=back_send.at[slot],
            recv_sem=back_recv.at[slot],
            device_id=device,
            device_id_type=MESH,
        )

    sends_w = jnp.logical_and(jnp.logical_and(core == 1, y == 0), has_on)
    takes_w = jnp.logical_and(jnp.logical_and(core == 0, y == 0), has_on)
    x_out = [copy(A0, X0, c, (own_on, y)) for c in range(chunks)]
    y_out = [copy(X0, Y0, c, (other, y)) for c in range(chunks)]
    z_core0 = [copy(A1, Z, c, (other_on, y)) for c in range(chunks)]
    z_core1 = [copy(A1, Z, c, (other, y)) for c in range(chunks)]
    w_out = [copy(A1, W, c, (other_on, y)) for c in range(chunks)]
    back = {
        A1: give(A1, (blk, y_back)), A2: give(A2, (blk, y_two)), X0: give(X0, (own_back, y)), B0: give(B0, (other, y)),
        Y0: give(Y0, (other_on, y)), Z: give(Z, (z_to, y_on)),
        W: give(W, (2 * wrap(t - 1, columns) + 1, groups - 1)),
    }

    small[2].wait()
    signs = (2 * sign_ref[...] - 1).astype(F32).astype(BF16)
    sent = []
    for c in range(chunks):
        loads[c].wait()
        here = pl.ds(c * part, part)
        x_in[here, :] = x_in[here, :] * signs

        def project(n, total):
            span = pl.ds(pl.multiple_of(n * 256, 256), 256)
            some = jnp.dot(x_in[here, :], table[:, span], preferred_element_type=F32)
            picked[:, span] = some
            return total + some[:, :128] * some[:, :128] + some[:, 128:] * some[:, 128:]

        total = lax.fori_loop(0, kept // 256, project, jnp.zeros((part, 128), F32))
        scale = lax.rsqrt(jnp.sum(total, axis=1, keepdims=True) + 1e-6)
        held[here, :] = (picked[...] * scale).astype(BF16)
        if c == 0:
            pl.semaphore_wait(barrier, 5 + jnp.where(has_on, 3, 0) + jnp.where(has_back, 1, 0))

        for target, device in ((A1, (blk, y_on)), (B0, (other, y))):
            out = copy(A0, target, c, device)
            out.start()
            sent.append(out)

        @pl.when(has_on)
        def _():
            x_out[c].start()

    tiles(A0, A0, own=True)
    for c in range(chunks):
        copy(A0, B0, c, (other, y)).wait_recv()

    @pl.when(core == 1)
    def _():
        tiles(A0, B0)

    for c in range(chunks):
        copy(A0, A1, c, (blk, y_on)).wait_recv()
        out = copy(A1, A2, c, (blk, y_on))
        out.start()
        sent.append(out)

        @pl.when(jnp.logical_and(core == 0, has_on))
        def _():
            z_core0[c].start()

        @pl.when(core == 1)
        def _():
            z_core1[c].start()

        @pl.when(sends_w)
        def _():
            w_out[c].start()

        @pl.when(has_back)
        def _():
            x_out[c].wait_recv()
            y_out[c].start()
            tiles(A0, X0, right_part=c)

        tiles(A1, A0, left_part=c)

    @pl.when(has_back)
    def _():
        tiles(A1, X0)

    @pl.when(has_on)
    def _():
        for c in range(chunks):
            y_out[c].wait_recv()

    @pl.when(core == 0)
    def _():
        tiles(A1, B0)

    @pl.when(jnp.logical_and(core == 0, has_on))
    def _():
        tiles(A0, Y0)

    @pl.when(jnp.logical_and(core == 1, has_on))
    def _():
        tiles(A1, Y0)

    @pl.when(takes_w)
    def _():
        for c in range(chunks):
            w_out[c].wait_recv()
        tiles(B0, W)
        close(B0)

    close(A0)
    close(A1)
    back[A1].start()
    for c in range(chunks):
        copy(A1, A2, c, (blk, y_on)).wait_recv()
        tiles(A2, A0, left_part=c)

        @pl.when(has_back)
        def _():
            tiles(A2, X0, left_part=c)

        @pl.when(jnp.logical_and(core == 0, has_on))
        def _():
            tiles(A2, Y0, left_part=c)

        @pl.when(core == 1)
        def _():
            tiles(A2, B0, left_part=c)

        @pl.when(has_z)
        def _():
            z_core1[c].wait_recv()
            tiles(A2, Z, left_part=c, right_part=c)
            for before in range(c):
                tiles(A2, Z, left_part=c, right_part=before)
                tiles(A2, Z, left_part=before, right_part=c)

    @pl.when(jnp.logical_and(jnp.logical_and(core == 1, has_z), y == groups - 1))
    def _():
        tiles(B0, Z)
        close(B0)

    close(A2)
    back[A2].start()
    back[B0].start()

    @pl.when(has_back)
    def _():
        back[X0].start()

    @pl.when(has_on)
    def _():
        back[Y0].start()

    @pl.when(has_z)
    def _():
        back[Z].start()

    @pl.when(takes_w)
    def _():
        back[W].start()

    best = lane_best[pl.ds(A0 * 8, 8), :]
    for slot in (A1, A2, B0):
        back[slot].wait_recv()
        best = jnp.maximum(best, landed[pl.ds(slot * 8, 8), :])
    lane_best[pl.ds(A0 * 8, 8), :] = best

    def take(condition, slot):
        @pl.when(condition)
        def _():
            back[slot].wait_recv()
            lane_best[pl.ds(A0 * 8, 8), :] = jnp.maximum(
                lane_best[pl.ds(A0 * 8, 8), :], landed[pl.ds(slot * 8, 8), :]
            )

    take(has_on, X0)
    take(has_on, Y0)
    take(jnp.logical_or(core == 1, t > 0), Z)
    take(jnp.logical_and(jnp.logical_and(core == 1, has_on), y == groups - 1), W)
    out_ref[...] = jnp.max(lane_best[pl.ds(A0 * 8, 8), :], axis=0, keepdims=True)

    for out in (*sent, back[A1], back[A2], back[B0]):
        out.wait_send()
    for condition, outs in (
        (has_on, x_out), (has_back, y_out), (jnp.logical_and(core == 0, has_on), z_core0), (core == 1, z_core1),
        (sends_w, w_out), (has_back, [back[X0]]), (has_on, [back[Y0]]), (has_z, [back[Z]]), (takes_w, [back[W]]),
    ):
        @pl.when(condition)
        def _():
            for out in outs:
                out.wait_send()


def solution(mesh):
    blocks, groups = mesh.shape["blk"], mesh.shape["grp"]
    chunks = 2

    def local(embeddings, cluster_sizes, sign_bits, sample_cols):
        rows, width = embeddings.shape
        kept = sample_cols.shape[0]
        vmem = pl.BlockSpec(memory_space=pltpu.VMEM)
        hbm = pl.BlockSpec(memory_space=pltpu.HBM)
        best = pl.pallas_call(
            functools.partial(kernel, blocks, groups, chunks),
            out_shape=jax.ShapeDtypeStruct((1, rows), F32),
            in_specs=[hbm] * 4,
            out_specs=vmem,
            scratch_shapes=[
                pltpu.VMEM((1, cluster_sizes.shape[0]), jnp.int32),
                pltpu.VMEM((1, width), jnp.int32),
                pltpu.VMEM((1, kept), jnp.int32),
                pltpu.VMEM((8 * rows, kept), BF16),
                pltpu.VMEM((rows, width), BF16),
                pltpu.VMEM((width, kept), BF16),
                pltpu.VMEM((rows // chunks, kept), F32),
                pltpu.VMEM((5 * rows, 128), F32),
                pltpu.VMEM((64, rows), F32),
                pltpu.VMEM((5 * rows, 128), F32),
                pltpu.VMEM((64, rows), F32),
                pltpu.VMEM((64, rows), F32),
                pltpu.SemaphoreType.DMA((chunks,)),
                pltpu.SemaphoreType.DMA((3,)),
                pltpu.SemaphoreType.DMA((KINDS, chunks)),
                pltpu.SemaphoreType.DMA((KINDS, chunks)),
                pltpu.SemaphoreType.DMA((KINDS,)),
                pltpu.SemaphoreType.DMA((KINDS,)),
            ],
            compiler_params=pltpu.CompilerParams(
                collective_id=0, has_side_effects=True, vmem_limit_bytes=60 * 1024 * 1024
            ),
        )(embeddings, cluster_sizes.reshape(1, -1), sign_bits.reshape(1, -1), sample_cols.reshape(1, -1))
        return best.reshape(rows)

    placed = (P(("blk", "grp"), None), P(), P(), P())
    return jax.shard_map(local, mesh=mesh, in_specs=placed, out_specs=P(("blk", "grp")), check_vma=False)
```

```python
import functools

import jax
import jax.numpy as jnp
from jax import lax
from jax.experimental import pallas as pl
from jax.experimental.pallas import tpu as pltpu
from jax.sharding import PartitionSpec as P

HB = 256
MESH = pl.DeviceIdType.MESH
F32 = jnp.float32
BF16 = jnp.bfloat16

A0, A1, A2, X0, B0, Y0, Z, W = range(8)
KINDS = 8


def parity_sign(bits):
    bits = bits ^ (bits >> 2)
    bits = bits ^ (bits >> 1)
    return (1 - 2 * (bits & 1)).astype(F32)


def kernel(blocks, groups, chunks, emb_ref, sizes_in, sign_in, cols_in, out_ref, sizes_ref, sign_ref, cols_ref, held, x_in,
           *rest):
    tables = rest[:-12]
    (picked, row_best, lane_best, row_id, lane_id, landed, load_sem, small_sem, send_sem, recv_sem, back_send,
     back_recv) = rest[-12:]
    rows, width = x_in.shape
    lanes = tables[0].shape[1]
    kept = lanes * len(tables)
    part = rows // chunks
    columns = blocks // 2
    blk = lax.axis_index("blk")
    y = lax.axis_index("grp")
    core = lax.rem(blk, 2)
    t = blk // 2
    step = 2 * core - 1

    def wrap(v, n):
        return lax.rem(v + 2 * n, n)

    y_on, y_back, y_two = wrap(y + step, groups), wrap(y - step, groups), wrap(y + 2, groups)
    t_on, t_back = wrap(t + step, columns), wrap(t - step, columns)
    own_on, own_back = 2 * t_on + core, 2 * t_back + core
    other, other_on = 2 * t + 1 - core, 2 * t_on + 1 - core
    z_to = 2 * wrap(t + core, columns) + 1 - core

    has_on = jnp.logical_and(t + step >= 0, t + step < columns)
    has_back = jnp.logical_and(t - step >= 0, t - step < columns)
    has_z = jnp.logical_or(core == 0, t < columns - 1)

    barrier = pltpu.get_barrier_semaphore()

    def greet(*devices):
        for device in devices:
            pl.semaphore_signal(barrier, inc=1, device_id=device, device_id_type=MESH)

    small = [
        pltpu.make_async_copy(source, target, small_sem.at[i])
        for i, (source, target) in enumerate(((cols_in, cols_ref), (sizes_in, sizes_ref), (sign_in, sign_ref)))
    ]
    for load in small:
        load.start()

    greet((blk, y_on), (blk, y_back), (blk, y_two), (other, y))

    @pl.when(core == 0)
    def _():
        greet((other, y_on))

    @pl.when(core == 1)
    def _():
        greet((other, y_back))

    @pl.when(has_on)
    def _():
        greet((own_on, y), (other_on, y))

    @pl.when(jnp.logical_and(has_on, core == 0))
    def _():
        greet((other_on, y_back))

    @pl.when(jnp.logical_and(has_on, core == 1))
    def _():
        greet((other_on, y_on))

    @pl.when(has_back)
    def _():
        greet((own_back, y))

    loads = [
        pltpu.make_async_copy(emb_ref.at[pl.ds(c * part, part)], x_in.at[pl.ds(c * part, part)], load_sem.at[c])
        for c in range(chunks)
    ]
    for load in loads:
        load.start()

    def fill(n):
        cols = cols_ref[:, n * lanes:(n + 1) * lanes]
        nibble = lax.broadcasted_iota(jnp.int32, (16, lanes), 0)
        low = parity_sign(nibble & (cols & 15))
        high = parity_sign(nibble & ((cols >> 4) & 15))
        table = jnp.concatenate([(low * high[u:u + 1, :]).astype(BF16) for u in range(16)], axis=0)
        for run in range(width // HB):
            chosen = jnp.broadcast_to(jnp.where((cols >> 8) == run, 1.0, 0.0), (16, lanes)).astype(BF16)
            tables[n][pl.ds(run * HB, HB), :] = table * jnp.concatenate([chosen] * 16, axis=0)

    def number(column, of_core, place):
        return (2 * column + of_core) * groups + place

    def name_clusters():
        n_clusters = sizes_ref.shape[1]
        at = lax.broadcasted_iota(jnp.int32, (n_clusters, n_clusters), 0)
        upto = lax.broadcasted_iota(jnp.int32, (n_clusters, n_clusters), 1)
        ends = jnp.sum(jnp.where(upto <= at, sizes_ref[...], 0), axis=1, keepdims=True)
        numbers = [
            number(t, core, y), number(t, core, y_back), number(t, core, y_two), number(t_back, core, y),
            number(t, 1 - core, y), number(t_on, 1 - core, y), number(wrap(t + core, columns), 1 - core, y_on),
            number(wrap(t - 1, columns), 1, groups - 1),
        ]
        for slot, block in enumerate(numbers):
            which = block * rows + lax.broadcasted_iota(jnp.int32, (n_clusters, rows), 1)
            ids = jnp.sum(jnp.where(ends <= which, 1.0, 0.0), axis=0, keepdims=True)
            lane_id[pl.ds(slot * 8, 8), :] = jnp.broadcast_to(ids, (8, rows))
            if slot in (A0, A1, A2, B0):
                row_id[pl.ds(slot * rows, rows), :] = jnp.broadcast_to(ids, (128, rows)).T


    def copy(source, target, c, device):
        return pltpu.make_async_remote_copy(
            src_ref=held.at[pl.ds(source * rows + c * part, part)],
            dst_ref=held.at[pl.ds(target * rows + c * part, part)],
            send_sem=send_sem.at[target, c],
            recv_sem=recv_sem.at[target, c],
            device_id=device,
            device_id_type=MESH,
        )

    def tile(left, left_at, count, right, right_at, lanes, own):
        rows_at = left * rows + left_at
        if not isinstance(rows_at, int):
            rows_at = pl.multiple_of(rows_at, 128)
        other_at = right * rows + right_at
        if not isinstance(other_at, int):
            other_at = pl.multiple_of(other_at, 128)
        scores = lax.dot_general(
            held[pl.ds(rows_at, count), :], held[pl.ds(other_at, lanes), :], (((1,), (1,)), ((), ())),
            preferred_element_type=F32,
        )
        left_ids = row_id[pl.ds(rows_at, count), :]
        best = row_best[pl.ds(rows_at, count), :]
        lane_row = right * 8 if isinstance(right, int) else pl.multiple_of(right * 8, 8)
        for j in range(lanes // 128):
            span = pl.ds(right_at + j * 128, 128)
            paired = left_ids == lane_id[pl.ds(lane_row, 8), span][0:1, :]
            if own:
                mine = left_at + lax.broadcasted_iota(jnp.int32, (count, 128), 0)
                theirs = right_at + j * 128 + lax.broadcasted_iota(jnp.int32, (count, 128), 1)
                paired = paired & (mine != theirs)
            masked = jnp.where(paired, scores[:, j * 128:(j + 1) * 128], -1.0)
            best = jnp.maximum(best, masked)
            if not own:
                lane_best[pl.ds(lane_row, 8), span] = jnp.maximum(
                    lane_best[pl.ds(lane_row, 8), span], jnp.max(masked.reshape(count // 8, 8, 128), axis=0)
                )
        row_best[pl.ds(rows_at, count), :] = best

    def tiles(left, right, left_parts=None, right_parts=None, own=False):
        left_from, left_to = (0, chunks) if left_parts is None else left_parts
        right_from, right_to = (0, chunks) if right_parts is None else right_parts
        for lc in range(left_from, left_to, 2):
            count = min(2, left_to - lc) * part
            for rc in range(right_from, right_to, 2):
                tile(left, lc * part, count, right, rc * part, min(2, right_to - rc) * part, own)

    def close(slot, first=0, last=chunks):
        span = pl.ds(first * part, (last - first) * part)
        turned = row_best[pl.ds(slot * rows + first * part, (last - first) * part), :].T
        lane_best[pl.ds(slot * 8, 8), span] = jnp.maximum(
            lane_best[pl.ds(slot * 8, 8), span], jnp.max(turned.reshape(16, 8, (last - first) * part), axis=0)
        )

    def give(slot, device):
        return pltpu.make_async_remote_copy(
            src_ref=lane_best.at[pl.ds(slot * 8, 8)],
            dst_ref=landed.at[pl.ds(slot * 8, 8)],
            send_sem=back_send.at[slot],
            recv_sem=back_recv.at[slot],
            device_id=device,
            device_id_type=MESH,
        )

    sends_w = jnp.logical_and(jnp.logical_and(core == 1, y == 0), has_on)
    takes_w = jnp.logical_and(jnp.logical_and(core == 0, y == 0), has_on)
    needs_far = jnp.logical_and(has_back, jnp.where(core == 1, y - groups // 2, groups // 2 - 1 - y) >= 0)
    edge_z = jnp.logical_and(jnp.logical_and(core == 1, has_z), y == groups - 1)
    x_out = [copy(A0, X0, c, (own_on, y)) for c in range(chunks)]
    y_out = [copy(X0, Y0, c, (other, y)) for c in range(chunks)]
    z_core0 = [copy(A1, Z, c, (other_on, y)) for c in range(chunks)]
    z_core1 = [copy(A1, Z, c, (other, y)) for c in range(chunks)]
    w_out = [copy(A1, W, c, (other_on, y)) for c in range(chunks)]
    back = {
        A1: give(A1, (blk, y_back)), A2: give(A2, (blk, y_two)), X0: give(X0, (own_back, y)), B0: give(B0, (other, y)),
        Y0: give(Y0, (other_on, y)), Z: give(Z, (z_to, y_on)),
        W: give(W, (2 * wrap(t - 1, columns) + 1, groups - 1)),
    }

    small[2].wait()
    signs = (2 * sign_ref[...] - 1).astype(F32).astype(BF16)
    sent = []
    small[0].wait()
    for c in range(chunks):
        loads[c].wait()
        here = pl.ds(c * part, part)
        flipped = x_in[here, :] * signs
        total = jnp.zeros((part, 128), F32)
        for n in range(len(tables)):
            if c == 0:
                fill(n)
            some = jnp.dot(flipped, tables[n][...], preferred_element_type=F32)
            picked[:, n * lanes:(n + 1) * lanes] = some
            for k in range(0, lanes, 128):
                total = total + some[:, k:k + 128] * some[:, k:k + 128]
        scale = lax.rsqrt(jnp.sum(total, axis=1, keepdims=True) + 1e-6)
        held[here, :] = (picked[...] * scale).astype(BF16)
        if c == 0:
            pl.semaphore_wait(barrier, 5 + jnp.where(has_on, 3, 0) + jnp.where(has_back, 1, 0))

        for target, device in ((A1, (blk, y_on)), (B0, (other, y))):
            out = copy(A0, target, c, device)
            out.start()
            sent.append(out)

        @pl.when(has_on)
        def _():
            x_out[c].start()

    row_best[...] = jnp.full_like(row_best, -1.0)
    lane_best[...] = jnp.full_like(lane_best, -1.0)
    small[1].wait()
    name_clusters()
    tiles(A0, A0, own=True)
    for c in range(chunks):
        copy(A0, B0, c, (other, y)).wait_recv()

    @pl.when(core == 1)
    def _():
        tiles(A0, B0)

    for c in range(chunks):
        copy(A0, A1, c, (blk, y_on)).wait_recv()
        out = copy(A1, A2, c, (blk, y_on))
        out.start()
        sent.append(out)

        @pl.when(jnp.logical_and(core == 0, has_on))
        def _():
            z_core0[c].start()

        @pl.when(core == 1)
        def _():
            z_core1[c].start()

        @pl.when(sends_w)
        def _():
            w_out[c].start()

        @pl.when(has_back)
        def _():
            x_out[c].wait_recv()
            y_out[c].start()

        if c % 2:
            tiles(A1, A0, left_parts=(c - 1, c + 1))

            @pl.when(has_back)
            def _():
                tiles(A0, X0, right_parts=(c - 1, c + 1))

    @pl.when(has_back)
    def _():
        tiles(A1, X0)

    @pl.when(has_on)
    def _():
        for c in range(chunks):
            y_out[c].wait_recv()

    @pl.when(core == 0)
    def _():
        tiles(A1, B0)

    @pl.when(jnp.logical_and(core == 0, has_on))
    def _():
        tiles(A0, Y0)

    @pl.when(jnp.logical_and(core == 1, has_on))
    def _():
        tiles(A1, Y0)

    close(A1)
    back[A1].start()

    @pl.when(jnp.logical_and(core == 0, jnp.logical_not(takes_w)))
    def _():
        back[B0].start()

    @pl.when(jnp.logical_and(core == 1, has_on))
    def _():
        back[Y0].start()

    for c in range(chunks):
        copy(A1, A2, c, (blk, y_on)).wait_recv()
        one = (c, c + 1)

        @pl.when(needs_far)
        def _():
            tiles(A2, X0, left_parts=one)

        @pl.when(jnp.logical_and(core == 0, has_on))
        def _():
            tiles(A2, Y0, left_parts=one)

        @pl.when(core == 1)
        def _():
            tiles(A2, B0, left_parts=one)

        if c == chunks - 1:

            @pl.when(has_back)
            def _():
                back[X0].start()

            @pl.when(jnp.logical_and(core == 0, has_on))
            def _():
                back[Y0].start()

            @pl.when(jnp.logical_and(core == 1, jnp.logical_not(edge_z)))
            def _():
                back[B0].start()

        tiles(A2, A0, left_parts=one)
        if c % 2:
            two = (c - 1, c + 1)

            @pl.when(has_z)
            def _():
                for k in range(*two):
                    z_core1[k].wait_recv()
                tiles(A2, Z, left_parts=(0, c + 1), right_parts=two)
                if c > 1:
                    tiles(A2, Z, left_parts=two, right_parts=(0, c - 1))

            if c == chunks - 1:
                close(A2)
                back[A2].start()

                @pl.when(jnp.logical_and(has_z, jnp.logical_not(edge_z)))
                def _():
                    back[Z].start()

            @pl.when(edge_z)
            def _():
                tiles(B0, Z, right_parts=two)

            @pl.when(takes_w)
            def _():
                for k in range(*two):
                    w_out[k].wait_recv()
                tiles(B0, W, right_parts=two)

    @pl.when(edge_z)
    def _():
        back[Z].start()
        close(B0)
        back[B0].start()

    @pl.when(takes_w)
    def _():
        back[W].start()
        close(B0)
        back[B0].start()

    close(A0)
    def take(condition, slot):
        @pl.when(condition)
        def _():
            back[slot].wait_recv()
            lane_best[pl.ds(A0 * 8, 8), :] = jnp.maximum(
                lane_best[pl.ds(A0 * 8, 8), :], landed[pl.ds(slot * 8, 8), :]
            )

    take(has_on, X0)
    take(has_on, Y0)
    for slot in (A1, B0, A2):
        back[slot].wait_recv()
    lane_best[pl.ds(A0 * 8, 8), :] = functools.reduce(
        jnp.maximum, [lane_best[pl.ds(A0 * 8, 8), :], *(landed[pl.ds(slot * 8, 8), :] for slot in (A1, B0, A2))]
    )
    take(jnp.logical_or(core == 1, t > 0), Z)
    take(jnp.logical_and(jnp.logical_and(core == 1, has_on), y == groups - 1), W)
    out_ref[...] = jnp.max(lane_best[pl.ds(A0 * 8, 8), :], axis=0, keepdims=True)

    for out in (*sent, back[A1], back[A2], back[B0]):
        out.wait_send()
    for condition, outs in (
        (has_on, x_out), (has_back, y_out), (jnp.logical_and(core == 0, has_on), z_core0), (core == 1, z_core1),
        (sends_w, w_out), (has_back, [back[X0]]), (has_on, [back[Y0]]), (has_z, [back[Z]]), (takes_w, [back[W]]),
    ):
        @pl.when(condition)
        def _():
            for out in outs:
                out.wait_send()


def solution(mesh):
    blocks, groups = mesh.shape["blk"], mesh.shape["grp"]
    chunks, lanes = 4, 256

    def local(embeddings, cluster_sizes, sign_bits, sample_cols):
        rows, width = embeddings.shape
        kept = sample_cols.shape[0]
        vmem = pl.BlockSpec(memory_space=pltpu.VMEM)
        hbm = pl.BlockSpec(memory_space=pltpu.HBM)
        best = pl.pallas_call(
            functools.partial(kernel, blocks, groups, chunks),
            out_shape=jax.ShapeDtypeStruct((1, rows), F32),
            in_specs=[hbm] * 4,
            out_specs=vmem,
            scratch_shapes=[
                pltpu.VMEM((1, cluster_sizes.shape[0]), jnp.int32),
                pltpu.VMEM((1, width), jnp.int32),
                pltpu.VMEM((1, kept), jnp.int32),
                pltpu.VMEM((8 * rows, kept), BF16),
                pltpu.VMEM((rows, width), BF16),
                *[pltpu.VMEM((width, lanes), BF16) for _ in range(kept // lanes)],
                pltpu.VMEM((rows // chunks, kept), F32),
                pltpu.VMEM((5 * rows, 128), F32),
                pltpu.VMEM((64, rows), F32),
                pltpu.VMEM((5 * rows, 128), F32),
                pltpu.VMEM((64, rows), F32),
                pltpu.VMEM((64, rows), F32),
                pltpu.SemaphoreType.DMA((chunks,)),
                pltpu.SemaphoreType.DMA((3,)),
                pltpu.SemaphoreType.DMA((KINDS, chunks)),
                pltpu.SemaphoreType.DMA((KINDS, chunks)),
                pltpu.SemaphoreType.DMA((KINDS,)),
                pltpu.SemaphoreType.DMA((KINDS,)),
            ],
            compiler_params=pltpu.CompilerParams(
                collective_id=0, has_side_effects=True, vmem_limit_bytes=60 * 1024 * 1024
            ),
        )(embeddings, cluster_sizes.reshape(1, -1), sign_bits.reshape(1, -1), sample_cols.reshape(1, -1))
        return best.reshape(rows)

    placed = (P(("blk", "grp"), None), P(), P(), P())
    return jax.shard_map(local, mesh=mesh, in_specs=placed, out_specs=P(("blk", "grp")), check_vma=False)
```

```python
import functools

import jax
import jax.numpy as jnp
from jax import lax
from jax.experimental import pallas as pl
from jax.experimental.pallas import tpu as pltpu
from jax.sharding import PartitionSpec as P

HB = 256
MESH = pl.DeviceIdType.MESH
F32 = jnp.float32
BF16 = jnp.bfloat16

A0, A1, A2, X0, B0, Y0, Z, W = range(8)
KINDS = 8


def parity_sign(bits):
    bits = bits ^ (bits >> 2)
    bits = bits ^ (bits >> 1)
    return (1 - 2 * (bits & 1)).astype(F32)


def kernel(blocks, groups, chunks, emb_ref, sizes_in, sign_in, cols_in, out_ref, sizes_ref, sign_ref, cols_ref, held, x_in,
           *rest):
    tables = rest[:-12]
    (picked, row_best, lane_best, row_id, lane_id, landed, load_sem, small_sem, send_sem, recv_sem, back_send,
     back_recv) = rest[-12:]
    rows, width = x_in.shape
    lanes = tables[0].shape[1]
    kept = lanes * len(tables)
    part = rows // chunks
    joint = 256 // part
    columns = blocks // 2
    blk = lax.axis_index("blk")
    y = lax.axis_index("grp")
    core = lax.rem(blk, 2)
    t = blk // 2
    step = 2 * core - 1

    def wrap(v, n):
        return lax.rem(v + 2 * n, n)

    y_on, y_back, y_two = wrap(y + step, groups), wrap(y - step, groups), wrap(y + 2, groups)
    t_on, t_back = wrap(t + step, columns), wrap(t - step, columns)
    own_on, own_back = 2 * t_on + core, 2 * t_back + core
    other, other_on = 2 * t + 1 - core, 2 * t_on + 1 - core
    z_to = 2 * wrap(t + core, columns) + 1 - core

    has_on = jnp.logical_and(t + step >= 0, t + step < columns)
    has_back = jnp.logical_and(t - step >= 0, t - step < columns)
    has_z = jnp.logical_or(core == 0, t < columns - 1)

    barrier = pltpu.get_barrier_semaphore()

    def greet(*devices):
        for device in devices:
            pl.semaphore_signal(barrier, inc=1, device_id=device, device_id_type=MESH)

    small = [
        pltpu.make_async_copy(source, target, small_sem.at[i])
        for i, (source, target) in enumerate(((cols_in, cols_ref), (sizes_in, sizes_ref), (sign_in, sign_ref)))
    ]
    for load in small:
        load.start()

    greet((blk, y_on), (blk, y_back), (other, y))

    @pl.when(has_on)
    def _():
        greet((own_on, y), (other_on, y))

    @pl.when(has_back)
    def _():
        greet((own_back, y))

    loads = [
        pltpu.make_async_copy(emb_ref.at[pl.ds(c * part, part)], x_in.at[pl.ds(c * part, part)], load_sem.at[c])
        for c in range(chunks)
    ]
    for load in loads:
        load.start()

    def fill(n):
        cols = cols_ref[:, n * lanes:(n + 1) * lanes]
        nibble = lax.broadcasted_iota(jnp.int32, (16, lanes), 0)
        low = parity_sign(nibble & (cols & 15))
        high = parity_sign(nibble & ((cols >> 4) & 15))
        table = jnp.concatenate([(low * high[u:u + 1, :]).astype(BF16) for u in range(16)], axis=0)
        for run in range(width // HB):
            chosen = jnp.broadcast_to(jnp.where((cols >> 8) == run, 1.0, 0.0), (16, lanes)).astype(BF16)
            tables[n][pl.ds(run * HB, HB), :] = table * jnp.concatenate([chosen] * 16, axis=0)

    def number(column, of_core, place):
        return (2 * column + of_core) * groups + place

    def name_clusters():
        n_clusters = sizes_ref.shape[1]
        at = lax.broadcasted_iota(jnp.int32, (n_clusters, n_clusters), 0)
        upto = lax.broadcasted_iota(jnp.int32, (n_clusters, n_clusters), 1)
        ends = jnp.sum(jnp.where(upto <= at, sizes_ref[...], 0), axis=1, keepdims=True)
        numbers = [
            number(t, core, y), number(t, core, y_back), number(t, core, y_two), number(t_back, core, y),
            number(t, 1 - core, y), number(t_on, 1 - core, y), number(wrap(t + core, columns), 1 - core, y_on),
            number(wrap(t - 1, columns), 1, groups - 1),
        ]
        for slot, block in enumerate(numbers):
            which = block * rows + lax.broadcasted_iota(jnp.int32, (n_clusters, rows), 1)
            ids = jnp.sum(jnp.where(ends <= which, 1.0, 0.0), axis=0, keepdims=True)
            lane_id[pl.ds(slot * 8, 8), :] = jnp.broadcast_to(ids, (8, rows))
            if slot in (A0, A1, A2, B0):
                row_id[pl.ds(slot * rows, rows), :] = jnp.broadcast_to(ids, (128, rows)).T


    def copy(source, target, c, device):
        return pltpu.make_async_remote_copy(
            src_ref=held.at[pl.ds(source * rows + c * part, part)],
            dst_ref=held.at[pl.ds(target * rows + c * part, part)],
            send_sem=send_sem.at[target, c],
            recv_sem=recv_sem.at[target, c],
            device_id=device,
            device_id_type=MESH,
        )

    def tile(left, left_at, count, right, right_at, lanes, own):
        rows_at = left * rows + left_at
        if not isinstance(rows_at, int):
            rows_at = pl.multiple_of(rows_at, 128)
        other_at = right * rows + right_at
        if not isinstance(other_at, int):
            other_at = pl.multiple_of(other_at, 128)
        scores = lax.dot_general(
            held[pl.ds(rows_at, count), :], held[pl.ds(other_at, lanes), :], (((1,), (1,)), ((), ())),
            preferred_element_type=F32,
        )
        left_ids = row_id[pl.ds(rows_at, count), :]
        best = row_best[pl.ds(rows_at, count), :]
        lane_row = right * 8 if isinstance(right, int) else pl.multiple_of(right * 8, 8)
        for j in range(lanes // 128):
            span = pl.ds(right_at + j * 128, 128)
            paired = left_ids == lane_id[pl.ds(lane_row, 8), span][0:1, :]
            if own:
                mine = left_at + lax.broadcasted_iota(jnp.int32, (count, 128), 0)
                theirs = right_at + j * 128 + lax.broadcasted_iota(jnp.int32, (count, 128), 1)
                paired = paired & (mine != theirs)
            masked = jnp.where(paired, scores[:, j * 128:(j + 1) * 128], -1.0)
            best = jnp.maximum(best, masked)
            if not own:
                lane_best[pl.ds(lane_row, 8), span] = jnp.maximum(
                    lane_best[pl.ds(lane_row, 8), span], jnp.max(masked.reshape(count // 8, 8, 128), axis=0)
                )
        row_best[pl.ds(rows_at, count), :] = best

    def tiles(left, right, left_parts=None, right_parts=None, own=False):
        left_from, left_to = (0, chunks) if left_parts is None else left_parts
        right_from, right_to = (0, chunks) if right_parts is None else right_parts
        for lc in range(left_from, left_to, joint):
            count = min(joint, left_to - lc) * part
            for rc in range(right_from, right_to, joint):
                tile(left, lc * part, count, right, rc * part, min(joint, right_to - rc) * part, own)

    def close(slot, first=0, last=chunks):
        span = pl.ds(first * part, (last - first) * part)
        turned = row_best[pl.ds(slot * rows + first * part, (last - first) * part), :].T
        lane_best[pl.ds(slot * 8, 8), span] = jnp.maximum(
            lane_best[pl.ds(slot * 8, 8), span], jnp.max(turned.reshape(16, 8, (last - first) * part), axis=0)
        )

    def give(slot, device):
        return pltpu.make_async_remote_copy(
            src_ref=lane_best.at[pl.ds(slot * 8, 8)],
            dst_ref=landed.at[pl.ds(slot * 8, 8)],
            send_sem=back_send.at[slot],
            recv_sem=back_recv.at[slot],
            device_id=device,
            device_id_type=MESH,
        )

    sends_w = jnp.logical_and(jnp.logical_and(core == 1, y == 0), has_on)
    takes_w = jnp.logical_and(jnp.logical_and(core == 0, y == 0), has_on)
    far = jnp.where(core == 1, y - groups // 2, groups // 2 - 1 - y) >= 0
    needs_far = jnp.logical_and(has_back, far)
    edge_z = jnp.logical_and(jnp.logical_and(core == 1, has_z), y == groups - 1)
    x_out = [copy(A0, X0, c, (own_on, y)) for c in range(chunks)]
    y_out = [copy(X0, Y0, c, (other, y)) for c in range(chunks)]
    z_core0 = [copy(A1, Z, c, (other_on, y)) for c in range(chunks)]
    z_core1 = [copy(A1, Z, c, (other, y)) for c in range(chunks)]
    w_out = [copy(A1, W, c, (other_on, y)) for c in range(chunks)]
    back = {
        A1: give(A1, (blk, y_back)), A2: give(A2, (blk, y_two)), X0: give(X0, (own_back, y)), B0: give(B0, (other, y)),
        Y0: give(Y0, (other_on, y)), Z: give(Z, (z_to, y_on)),
        W: give(W, (2 * wrap(t - 1, columns) + 1, groups - 1)),
    }

    small[2].wait()
    signs = (2 * sign_ref[...] - 1).astype(F32).astype(BF16)
    sent = []
    small[0].wait()
    for c in range(chunks):
        loads[c].wait()
        here = pl.ds(c * part, part)
        flipped = x_in[here, :] * signs
        total = jnp.zeros((part, 128), F32)
        for n in range(len(tables)):
            if c == 0:
                fill(n)
            some = jnp.dot(flipped, tables[n][...], preferred_element_type=F32)
            picked[:, n * lanes:(n + 1) * lanes] = some
            for k in range(0, lanes, 128):
                total = total + some[:, k:k + 128] * some[:, k:k + 128]
        scale = lax.rsqrt(jnp.sum(total, axis=1, keepdims=True) + 1e-6)
        held[here, :] = (picked[...] * scale).astype(BF16)
        if c == 0:
            pl.semaphore_wait(barrier, 3 + jnp.where(has_on, 2, 0) + jnp.where(has_back, 1, 0))

        @pl.when(has_on)
        def _():
            x_out[c].start()

        for target, device in ((A1, (blk, y_on)), (B0, (other, y))):
            out = copy(A0, target, c, device)
            out.start()
            sent.append(out)

    row_best[...] = jnp.full_like(row_best, -1.0)
    lane_best[...] = jnp.full_like(lane_best, -1.0)
    small[1].wait()
    name_clusters()
    tiles(A0, A0, own=True)
    for c in range(chunks):
        copy(A0, B0, c, (other, y)).wait_recv()

    @pl.when(core == 1)
    def _():
        tiles(A0, B0)

    for c in range(chunks):
        copy(A0, A1, c, (blk, y_on)).wait_recv()
        out = copy(A1, A2, c, (blk, y_on))
        out.start()
        sent.append(out)

        @pl.when(jnp.logical_and(core == 0, has_on))
        def _():
            z_core0[c].start()

        @pl.when(core == 1)
        def _():
            z_core1[c].start()

        @pl.when(sends_w)
        def _():
            w_out[c].start()

        @pl.when(has_back)
        def _():
            x_out[c].wait_recv()
            y_out[c].start()

        if c % joint == joint - 1:
            two = (c - joint + 1, c + 1)
            tiles(A1, A0, left_parts=two)

            @pl.when(has_back)
            def _():
                tiles(A0, X0, right_parts=two)

    @pl.when(has_back)
    def _():
        tiles(A1, X0)

    @pl.when(has_on)
    def _():
        for c in range(chunks):
            y_out[c].wait_recv()

    @pl.when(core == 0)
    def _():
        tiles(A1, B0)

    @pl.when(jnp.logical_and(core == 0, has_on))
    def _():
        tiles(A0, Y0)

    @pl.when(jnp.logical_and(core == 1, has_on))
    def _():
        tiles(A1, Y0)

    close(A1)
    back[A1].start()

    @pl.when(jnp.logical_and(core == 0, jnp.logical_not(takes_w)))
    def _():
        back[B0].start()

    @pl.when(jnp.logical_and(core == 1, has_on))
    def _():
        back[Y0].start()

    for c in range(chunks):
        copy(A1, A2, c, (blk, y_on)).wait_recv()
        one = (c, c + 1)

        @pl.when(needs_far)
        def _():
            tiles(A2, X0, left_parts=one)

        @pl.when(jnp.logical_and(core == 0, has_on))
        def _():
            tiles(A2, Y0, left_parts=one)

        @pl.when(core == 1)
        def _():
            tiles(A2, B0, left_parts=one)

        if c == chunks - 1:

            @pl.when(has_back)
            def _():
                back[X0].start()

            @pl.when(jnp.logical_and(core == 0, has_on))
            def _():
                back[Y0].start()

            @pl.when(jnp.logical_and(core == 1, jnp.logical_not(edge_z)))
            def _():
                back[B0].start()

        @pl.when(jnp.logical_not(far))
        def _():
            tiles(A2, A0, left_parts=one)

        if c % joint == joint - 1:
            two = (c - joint + 1, c + 1)

            @pl.when(has_z)
            def _():
                for k in range(*two):
                    z_core1[k].wait_recv()

            @pl.when(edge_z)
            def _():
                tiles(B0, Z, right_parts=two)

            @pl.when(has_z)
            def _():
                tiles(A2, Z, left_parts=(0, c + 1), right_parts=two)
                if c >= joint:
                    tiles(A2, Z, left_parts=two, right_parts=(0, c - joint + 1))

            if c == chunks - 1:

                @pl.when(has_z)
                def _():
                    back[Z].start()

                close(A2)
                back[A2].start()

            @pl.when(takes_w)
            def _():
                for k in range(*two):
                    w_out[k].wait_recv()
                tiles(B0, W, right_parts=two)

    @pl.when(edge_z)
    def _():
        close(B0)
        back[B0].start()

    @pl.when(takes_w)
    def _():
        back[W].start()
        close(B0)
        back[B0].start()

    close(A0)
    def take(condition, slot):
        @pl.when(condition)
        def _():
            back[slot].wait_recv()
            lane_best[pl.ds(A0 * 8, 8), :] = jnp.maximum(
                lane_best[pl.ds(A0 * 8, 8), :], landed[pl.ds(slot * 8, 8), :]
            )

    take(has_on, X0)
    take(has_on, Y0)
    for slot in (A1, B0, A2):
        back[slot].wait_recv()
    lane_best[pl.ds(A0 * 8, 8), :] = functools.reduce(
        jnp.maximum, [lane_best[pl.ds(A0 * 8, 8), :], *(landed[pl.ds(slot * 8, 8), :] for slot in (A1, B0, A2))]
    )
    take(jnp.logical_or(core == 1, t > 0), Z)
    take(jnp.logical_and(jnp.logical_and(core == 1, has_on), y == groups - 1), W)
    out_ref[...] = jnp.max(lane_best[pl.ds(A0 * 8, 8), :], axis=0, keepdims=True)

    for out in (*sent, back[A1], back[A2], back[B0]):
        out.wait_send()
    for condition, outs in (
        (has_on, x_out), (has_back, y_out), (jnp.logical_and(core == 0, has_on), z_core0), (core == 1, z_core1),
        (sends_w, w_out), (has_back, [back[X0]]), (has_on, [back[Y0]]), (has_z, [back[Z]]), (takes_w, [back[W]]),
    ):
        @pl.when(condition)
        def _():
            for out in outs:
                out.wait_send()


def solution(mesh):
    blocks, groups = mesh.shape["blk"], mesh.shape["grp"]
    chunks, lanes = 4, 256

    def local(embeddings, cluster_sizes, sign_bits, sample_cols):
        rows, width = embeddings.shape
        kept = sample_cols.shape[0]
        vmem = pl.BlockSpec(memory_space=pltpu.VMEM)
        hbm = pl.BlockSpec(memory_space=pltpu.HBM)
        best = pl.pallas_call(
            functools.partial(kernel, blocks, groups, chunks),
            out_shape=jax.ShapeDtypeStruct((1, rows), F32),
            in_specs=[hbm] * 4,
            out_specs=vmem,
            scratch_shapes=[
                pltpu.VMEM((1, cluster_sizes.shape[0]), jnp.int32),
                pltpu.VMEM((1, width), jnp.int32),
                pltpu.VMEM((1, kept), jnp.int32),
                pltpu.VMEM((8 * rows, kept), BF16),
                pltpu.VMEM((rows, width), BF16),
                *[pltpu.VMEM((width, lanes), BF16) for _ in range(kept // lanes)],
                pltpu.VMEM((rows // chunks, kept), F32),
                pltpu.VMEM((5 * rows, 128), F32),
                pltpu.VMEM((64, rows), F32),
                pltpu.VMEM((5 * rows, 128), F32),
                pltpu.VMEM((64, rows), F32),
                pltpu.VMEM((64, rows), F32),
                pltpu.SemaphoreType.DMA((chunks,)),
                pltpu.SemaphoreType.DMA((3,)),
                pltpu.SemaphoreType.DMA((KINDS, chunks)),
                pltpu.SemaphoreType.DMA((KINDS, chunks)),
                pltpu.SemaphoreType.DMA((KINDS,)),
                pltpu.SemaphoreType.DMA((KINDS,)),
            ],
            compiler_params=pltpu.CompilerParams(
                collective_id=0, has_side_effects=True, vmem_limit_bytes=60 * 1024 * 1024
            ),
        )(embeddings, cluster_sizes.reshape(1, -1), sign_bits.reshape(1, -1), sample_cols.reshape(1, -1))
        return best.reshape(rows)

    placed = (P(("blk", "grp"), None), P(), P(), P())
    return jax.shard_map(local, mesh=mesh, in_specs=placed, out_specs=P(("blk", "grp")), check_vma=False)
```
